32 devices in a mesh: dp: 8 (over y, x, core), width: 4 (over z).
Axes of the slice: x: 2, y: 2, z: 4, core: 2. Of those that a mesh axis runs over, the one named last changes fastest.
Arguments:
- hidden_inputs: bfloat16 [16, 2048, 14336], P('dp', None, 'width'), may hold values from -6 to 6
- output_grads: bfloat16 [16, 2048, 4096], P('dp'), may hold values from -6 to 6
- lengths: int32 [16], P('dp'), may hold values from 256 to 2048, as said below
- in_proj: bfloat16 [64, 14336], P(None, 'width'), may hold values from -0.046875 to 0.046875
- out_proj: bfloat16 [64, 4096], replicated, may hold values from -0.09375 to 0.09375
- query_sketches: bfloat16 [512, 4096], P(None, 'dp'), may hold values from -0.001953125 to 0.001953125
Outputs:
- scores: float32 [16, 512], P('dp')
The draws below stay inside these ranges and needn't reach their ends.
Inputs may be any that keep to these rules, and one draw needn't show every extreme that they name: `lengths`: some trace has all 2048 tokens valid.
All inputs are finite; a program needn't handle non-finite values.
Results may differ from the reference program's by a relative error of at most 0.0029.
Values may be sent and summed in bfloat16 or wider, within the bound.
No kernel may reach another device: no remote copies, remote signals or barrier semaphores. Data moves between devices by JAX's collectives and lax.ppermute only.
A program may use at most 128 MiB of HBM per device.

```python
import jax
import jax.numpy as jnp
from jax import lax

D = 4096
FF = 14336
RANK = 64
LEN = 2048
QUERIES = 512
TRACES = 16
SK = 4096


def draw_lengths(key, part):
    drawn_lengths = jax.random.randint(key, (TRACES,), LEN // 8, LEN + 1)
    full_index = jax.random.randint(jax.random.fold_in(key, 7), (), 0, TRACES)
    return jnp.where(jnp.arange(TRACES) == full_index, LEN, drawn_lengths).astype(jnp.int32)


def block_scale(rng, dims, pieces, least, top_value):
    level, own = 1.0, jax.random.fold_in(rng, 6)
    for position, parts in pieces:
        steps = jnp.exp(jax.random.uniform(jax.random.fold_in(own, position), (parts,), jnp.float32, least / len(pieces), top_value / len(pieces)))
        level = level * jnp.repeat(steps, dims[position] // parts).reshape([-1 if axis == position else 1 for axis in range(len(dims))])
    return level


def bell_draw(key, dims, width, bound, shards=(), kind=jnp.bfloat16):
    result = width * jax.random.normal(key, dims, jnp.float32)
    if shards:
        result = result * block_scale(key, dims, shards, -0.22, 0.18)
    return jnp.clip(result, -bound, bound).astype(kind)


def setup_inputs(seed: int = 0) -> dict:
    streams_of = jax.random.split(jax.random.key(seed), 7)
    hidden_inputs = bell_draw(streams_of[0], (TRACES, LEN, FF), 1.0, 6.0, ((0, 8), (2, 4)))
    output_grads = bell_draw(streams_of[1], (TRACES, LEN, D), 1.0, 6.0, ((0, 8),))
    lengths = draw_lengths(jax.random.fold_in(streams_of[6], 71), 0)
    in_proj = bell_draw(streams_of[3], (RANK, FF), FF ** -0.5, 0.046875, ((1, 4),))
    out_proj = bell_draw(streams_of[4], (RANK, D), D ** -0.5, 0.09375)
    query_sketches = bell_draw(streams_of[5], (QUERIES, SK), (SK * LEN) ** -0.5, 0.001953125, ((1, 8),))
    return {"hidden_inputs": hidden_inputs, "output_grads": output_grads, "lengths": lengths, "in_proj": in_proj, "out_proj": out_proj, "query_sketches": query_sketches}


def reference(hidden_inputs, output_grads, lengths, in_proj, out_proj, query_sketches):
    positions = jnp.arange(LEN, dtype=jnp.int32)

    def one_trace(items):
        hid_rows, grad_rows, count_len = items
        in_side = lax.dot_general(hid_rows, in_proj, (((1,), (1,)), ((), ())), preferred_element_type=jnp.float32)
        out_side = lax.dot_general(grad_rows, out_proj, (((1,), (1,)), ((), ())), preferred_element_type=jnp.float32)
        valid_tokens = (positions < count_len).astype(jnp.float32)
        out_side = out_side * valid_tokens[:, None]
        sketch = lax.dot_general(in_side, out_side, (((0,), (0,)), ((), ())), precision=lax.Precision.HIGHEST)
        return sketch.reshape(RANK * RANK)

    sketches = lax.map(one_trace, (hidden_inputs, output_grads, lengths))
    sketch_low = sketches.astype(jnp.bfloat16)
    return lax.dot_general(sketch_low, query_sketches, (((1,), (1,)), ((), ())), preferred_element_type=jnp.float32)
```

```python
import functools

import jax
import jax.numpy as jnp
from jax import lax
from jax.experimental import pallas as pl
from jax.experimental.pallas import tpu as pltpu
from jax.sharding import PartitionSpec as P

GRAN = 128
PAIR = 2
RING = 12

NT = (((1,), (1,)), ((), ()))
TN = (((0,), (0,)), ((), ()))


def split_bf16(value):
    high = value.astype(jnp.bfloat16)
    low = (value - high.astype(jnp.float32)).astype(jnp.bfloat16)
    return high, low


def sketch_kernel(
    lengths_hbm, hidden, grads, in_hbm, out_hbm, packed, hid_buf, grad_buf, in_proj, out_proj, lengths, in_last, out_last, total_ref, sems, once
):
    traces, length_dev, _ = hidden.shape
    rank = in_hbm.shape[0]

    def copies(slot, trace, row):
        rows = pl.ds(row, GRAN)
        return (
            pltpu.make_async_copy(hidden.at[trace, rows], hid_buf.at[slot], sems.at[0, slot]),
            pltpu.make_async_copy(grads.at[trace, rows], grad_buf.at[slot], sems.at[1, slot]),
        )

    fetch = [
        pltpu.make_async_copy(lengths_hbm, lengths, once.at[0]),
        pltpu.make_async_copy(in_hbm, in_proj.at[pl.ds(0, rank)], once.at[1]),
        pltpu.make_async_copy(out_hbm, out_proj.at[pl.ds(0, rank)], once.at[2]),
    ]
    for copy in fetch:
        copy.start()
    for index in range(PAIR):
        for copy in copies(index, 0, index * GRAN):
            copy.start()
    fetch[0].wait()
    counts = [jnp.minimum(lengths[i], length_dev) for i in range(traces)]
    firsts, total = [], 0
    for i in range(traces):
        firsts.append(total)
        total = total + (counts[i] + GRAN - 1) // GRAN

    def locate(index):
        trace, first, count = 0, 0, counts[0]
        for i in range(1, traces):
            later = index >= firsts[i]
            trace = jnp.where(later, i, trace)
            first = jnp.where(later, firsts[i], first)
            count = jnp.where(later, counts[i], count)
        return trace, pl.multiple_of((index - first) * GRAN, GRAN), count

    def start(index):
        @pl.when(index < total)
        def _():
            trace, row, _ = locate(index)
            for copy in copies(lax.rem(index, RING), trace, row):
                copy.start()

    for index in range(PAIR, RING):
        start(index)
    total_ref[...] = jnp.zeros_like(total_ref)
    in_last[...] = jnp.zeros_like(in_last)
    out_last[...] = jnp.zeros_like(out_last)
    for copy in fetch[1:]:
        copy.wait()
    in_proj[rank:] = in_proj[:rank]
    for i in range(1, traces):
        out_proj[i * rank : (i + 1) * rank] = out_proj[:rank]

    def project(index, parts):
        for part in range(parts):
            trace, row, _ = locate(index + part)
            for copy in copies(lax.rem(index + part, RING), trace, row):
                copy.wait()
        slots = pl.ds(lax.rem(index, RING), parts)
        hid_rows = hid_buf[slots].reshape(parts * GRAN, hid_buf.shape[2])
        grad_rows = grad_buf[slots].reshape(parts * GRAN, grad_buf.shape[2])
        in_side = lax.dot_general(hid_rows, in_proj[...], NT, preferred_element_type=jnp.float32)
        out_side = lax.dot_general(grad_rows, out_proj[...], NT, preferred_element_type=jnp.float32)
        return in_side, out_side

    def add(index, parts, in_side, out_side):
        block = lax.broadcasted_iota(jnp.int32, (GRAN, traces * rank), 1) // rank
        token = lax.broadcasted_iota(jnp.int32, (GRAN, traces * rank), 0)
        kept = []
        for part in range(parts):
            trace, row, count = locate(index + part)
            kept.append((block == trace) & (token + row < count))
        out_side = jnp.where(jnp.concatenate(kept, axis=0), out_side, 0.0)
        out_high, out_low = split_bf16(out_side)
        high = in_side.astype(jnp.bfloat16).astype(jnp.float32)
        first = lax.broadcasted_iota(jnp.int32, in_side.shape, 1) < rank
        both = jnp.where(first, high, in_side - high).astype(jnp.bfloat16)
        total_ref[...] += lax.dot_general(
            jnp.concatenate([both, both], axis=0),
            jnp.concatenate([out_high, out_low], axis=0),
            TN,
            preferred_element_type=jnp.float32,
        )

    def body(step, carry):
        index = step * PAIR
        in_before, out_before = in_last[...], out_last[...]
        in_side, out_side = project(index, PAIR)
        add(index - PAIR, PAIR, in_before, out_before)
        in_last[...] = in_side
        out_last[...] = out_side
        for part in range(PAIR):
            start(index + part + RING)
        return carry

    pairs = total // PAIR
    lax.fori_loop(0, pairs, body, 0)

    @pl.when(total % PAIR == 0)
    def _():
        add((pairs - 1) * PAIR, PAIR, in_last[...], out_last[...])

    @pl.when(total % PAIR != 0)
    def _():
        in_side, out_side = project(pairs * PAIR, 1)
        add((pairs - 1) * PAIR, PAIR, in_last[...], out_last[...])
        add(pairs * PAIR, 1, in_side, out_side)

    packed[...] = total_ref[:rank] + total_ref[rank:]


def local_sketches(lengths, hidden, grads, in_proj, out_proj):
    traces, length_dev, width_dev = hidden.shape
    rank, model = out_proj.shape
    rows = traces * length_dev
    return pl.pallas_call(
        sketch_kernel,
        out_shape=jax.ShapeDtypeStruct((rank, traces * rank), jnp.float32),
        in_specs=[pl.BlockSpec(memory_space=pltpu.HBM)] * 5,
        out_specs=pl.BlockSpec(memory_space=pltpu.VMEM),
        scratch_shapes=[
            pltpu.VMEM((RING, GRAN, width_dev), jnp.bfloat16),
            pltpu.VMEM((RING, GRAN, model), jnp.bfloat16),
            pltpu.VMEM((2 * rank, width_dev), jnp.bfloat16),
            pltpu.VMEM((traces * rank, model), jnp.bfloat16),
            pltpu.SMEM((traces,), jnp.int32),
            pltpu.VMEM((PAIR * GRAN, 2 * rank), jnp.float32),
            pltpu.VMEM((PAIR * GRAN, traces * rank), jnp.float32),
            pltpu.VMEM((2 * rank, traces * rank), jnp.float32),
            pltpu.SemaphoreType.DMA((2, RING)),
            pltpu.SemaphoreType.DMA((3,)),
        ],
        compiler_params=pltpu.CompilerParams(vmem_limit_bytes=40 << 20),
        cost_estimate=pl.CostEstimate(
            flops=2 * rows * rank * (width_dev + model),
            bytes_accessed=2 * rows * (width_dev + model),
            transcendentals=0,
        ),
        name="sketches",
    )(*(pltpu.with_memory_space_constraint(value, pltpu.HBM) for value in (lengths, hidden, grads, in_proj, out_proj)))


def score_kernel(traces, chip, first, second, *rest):
    pieces, (own_out, other_out) = rest[:-2], rest[-2:]
    rank = first.shape[2] // traces
    entries = pieces[0].shape[1]
    depth = entries // rank
    lane = lax.broadcasted_iota(jnp.int32, (depth, entries), 1) // rank
    diagonal = lane == lax.broadcasted_iota(jnp.int32, (depth, entries), 0)
    total = None
    for mask, piece in enumerate(pieces):
        rows = pl.ds(pl.multiple_of((chip[0] ^ mask) * depth, depth), depth)
        blocks = []
        for owner in range(2):
            values = first[owner, rows] + second[owner, rows]
            for trace in range(traces):
                wide = jnp.concatenate([values[:, trace * rank : (trace + 1) * rank]] * depth, axis=1)
                blocks.append(jnp.where(diagonal, wide, 0.0))
        high, low = split_bf16(jnp.concatenate(blocks, axis=0))
        left = jnp.concatenate([high, low], axis=0)
        term = lax.dot_general(left, piece[...], NT, preferred_element_type=jnp.float32)
        total = term if total is None else total + term
    half = total.shape[0] // 2
    total = total[:half] + total[half:]
    sums = jnp.sum(total.reshape(2 * traces, depth, total.shape[1]), axis=1)
    own_out[...] = sums[:traces]
    other_out[...] = sums[traces:]


def exchange(value, axis, size, mask):
    return lax.ppermute(value, axis, [(i, i ^ mask) for i in range(size)])


def per_device(dp, width, hidden_inputs, output_grads, lengths, in_proj, out_proj, query_sketches):
    traces, _, _ = hidden_inputs.shape
    queries, entries = query_sketches.shape
    rank = in_proj.shape[0]
    depth = entries // rank
    place, column = lax.axis_index("dp"), lax.axis_index("width")
    core, chip, half = place & 1, place >> 1, column & 1
    part = lax.dynamic_slice_in_dim(query_sketches, half * (queries // 2), queries // 2, 0)
    pieces = [part] + [exchange(part, "dp", dp, 2 * mask) for mask in range(1, dp // 2)]

    packed = local_sketches(lengths, hidden_inputs, output_grads, in_proj, out_proj)
    by_core = packed.reshape(dp // 2, 2, depth, traces * rank)
    even = by_core[:, 0].reshape(rank // 2, traces * rank)
    odd = by_core[:, 1].reshape(rank // 2, traces * rank)
    keep = jnp.where(core == 0, even, odd)
    got = exchange(jnp.where(core == 0, odd, even), "dp", dp, 1)
    mine = jnp.stack([keep, got])
    theirs = exchange(mine, "width", width, 1)

    scores = jax.ShapeDtypeStruct((traces, queries // 2), jnp.float32)
    vmem = pl.BlockSpec(memory_space=pltpu.VMEM)
    own, other = pl.pallas_call(
        functools.partial(score_kernel, traces),
        out_shape=(scores, scores),
        in_specs=[pl.BlockSpec(memory_space=pltpu.SMEM)] + [vmem] * (2 + len(pieces)),
        out_specs=(vmem, vmem),
        compiler_params=pltpu.CompilerParams(vmem_limit_bytes=24 << 20),
        name="scores",
    )(chip.astype(jnp.int32).reshape(1), mine, theirs, *pieces)
    partial = own + exchange(other, "dp", dp, 1)
    same, across = partial, None
    for mask in range(1, width):
        came = exchange(partial, "width", width, mask)
        if mask % 2 == 0:
            same = same + came
        else:
            across = came if across is None else across + came
    low = jnp.where(half == 0, same, across)
    high = jnp.where(half == 0, across, same)
    return jnp.concatenate([low, high], axis=1)


def solution(mesh):
    return jax.shard_map(
        functools.partial(per_device, mesh.shape["dp"], mesh.shape["width"]),
        mesh=mesh,
        in_specs=(
            P("dp", None, "width"),
            P("dp", None, None),
            P("dp"),
            P(None, "width"),
            P(),
            P(None, "dp"),
        ),
        out_specs=P("dp", None),
        check_vma=False,
    )
```

```python
import functools

import jax
import jax.numpy as jnp
from jax import lax
from jax.experimental import pallas as pl
from jax.experimental.pallas import tpu as pltpu
from jax.sharding import PartitionSpec as P

GRAN = 128
PAIR = 2
RING = 12

NT = (((1,), (1,)), ((), ()))
TN = (((0,), (0,)), ((), ()))


def split_bf16(value):
    high = value.astype(jnp.bfloat16)
    low = (value - high.astype(jnp.float32)).astype(jnp.bfloat16)
    return high, low


def sketch_kernel(
    lengths_hbm, hidden, grads, in_hbm, out_hbm, packed, hid_buf, grad_buf, in_proj, out_proj, lengths, in_last, out_last, total_ref, sems, once
):
    traces, length_dev, _ = hidden.shape
    rank = in_hbm.shape[0]

    def copies(slot, trace, row):
        rows = pl.ds(row, GRAN)
        return (
            pltpu.make_async_copy(hidden.at[trace, rows], hid_buf.at[slot], sems.at[0, slot]),
            pltpu.make_async_copy(grads.at[trace, rows], grad_buf.at[slot], sems.at[1, slot]),
        )

    fetch = [
        pltpu.make_async_copy(lengths_hbm, lengths, once.at[0]),
        pltpu.make_async_copy(in_hbm, in_proj.at[pl.ds(0, rank)], once.at[1]),
        pltpu.make_async_copy(out_hbm, out_proj.at[pl.ds(0, rank)], once.at[2]),
    ]
    for copy in fetch:
        copy.start()
    for index in range(PAIR):
        for copy in copies(index, 0, index * GRAN):
            copy.start()
    fetch[0].wait()
    counts = [jnp.minimum(lengths[i], length_dev) for i in range(traces)]
    firsts, total = [], 0
    for i in range(traces):
        firsts.append(total)
        total = total + (counts[i] + GRAN - 1) // GRAN

    def locate(index):
        trace, first, count = 0, 0, counts[0]
        for i in range(1, traces):
            later = index >= firsts[i]
            trace = jnp.where(later, i, trace)
            first = jnp.where(later, firsts[i], first)
            count = jnp.where(later, counts[i], count)
        return trace, pl.multiple_of((index - first) * GRAN, GRAN), count

    def start(index):
        @pl.when(index < total)
        def _():
            trace, row, _ = locate(index)
            for copy in copies(lax.rem(index, RING), trace, row):
                copy.start()

    for index in range(PAIR, RING):
        start(index)
    total_ref[...] = jnp.zeros_like(total_ref)
    in_last[...] = jnp.zeros_like(in_last)
    out_last[...] = jnp.zeros_like(out_last)
    for copy in fetch[1:]:
        copy.wait()
    in_proj[rank:] = in_proj[:rank]
    for i in range(1, traces):
        out_proj[i * rank : (i + 1) * rank] = out_proj[:rank]

    def project(index, parts):
        for part in range(parts):
            trace, row, _ = locate(index + part)
            for copy in copies(lax.rem(index + part, RING), trace, row):
                copy.wait()
        slots = pl.ds(lax.rem(index, RING), parts)
        hid_rows = hid_buf[slots].reshape(parts * GRAN, hid_buf.shape[2])
        grad_rows = grad_buf[slots].reshape(parts * GRAN, grad_buf.shape[2])
        in_side = lax.dot_general(hid_rows, in_proj[...], NT, preferred_element_type=jnp.float32)
        out_side = lax.dot_general(grad_rows, out_proj[...], NT, preferred_element_type=jnp.float32)
        return in_side, out_side

    def add(index, parts, in_side, out_side):
        block = lax.broadcasted_iota(jnp.int32, (GRAN, traces * rank), 1) // rank
        token = lax.broadcasted_iota(jnp.int32, (GRAN, traces * rank), 0)
        kept = []
        for part in range(parts):
            trace, row, count = locate(index + part)
            kept.append((block == trace) & (token + row < count))
        out_side = jnp.where(jnp.concatenate(kept, axis=0), out_side, 0.0)
        out_high, out_low = split_bf16(out_side)
        high = in_side.astype(jnp.bfloat16).astype(jnp.float32)
        first = lax.broadcasted_iota(jnp.int32, in_side.shape, 1) < rank
        both = jnp.where(first, high, in_side - high).astype(jnp.bfloat16)
        total_ref[...] += lax.dot_general(
            jnp.concatenate([both, both], axis=0),
            jnp.concatenate([out_high, out_low], axis=0),
            TN,
            preferred_element_type=jnp.float32,
        )

    def body(step, carry):
        index = step * PAIR
        in_before, out_before = in_last[...], out_last[...]
        in_side, out_side = project(index, PAIR)
        add(index - PAIR, PAIR, in_before, out_before)
        in_last[...] = in_side
        out_last[...] = out_side
        for part in range(PAIR):
            start(index + part + RING)
        return carry

    pairs = total // PAIR
    lax.fori_loop(0, pairs, body, 0)

    @pl.when(total % PAIR == 0)
    def _():
        add((pairs - 1) * PAIR, PAIR, in_last[...], out_last[...])

    @pl.when(total % PAIR != 0)
    def _():
        in_side, out_side = project(pairs * PAIR, 1)
        add((pairs - 1) * PAIR, PAIR, in_last[...], out_last[...])
        add(pairs * PAIR, 1, in_side, out_side)

    packed[...] = total_ref[:rank] + total_ref[rank:]


def local_sketches(lengths, hidden, grads, in_proj, out_proj):
    traces, length_dev, width_dev = hidden.shape
    rank, model = out_proj.shape
    rows = traces * length_dev
    return pl.pallas_call(
        sketch_kernel,
        out_shape=jax.ShapeDtypeStruct((rank, traces * rank), jnp.float32),
        in_specs=[pl.BlockSpec(memory_space=pltpu.HBM)] * 5,
        out_specs=pl.BlockSpec(memory_space=pltpu.VMEM),
        scratch_shapes=[
            pltpu.VMEM((RING, GRAN, width_dev), jnp.bfloat16),
            pltpu.VMEM((RING, GRAN, model), jnp.bfloat16),
            pltpu.VMEM((2 * rank, width_dev), jnp.bfloat16),
            pltpu.VMEM((traces * rank, model), jnp.bfloat16),
            pltpu.SMEM((traces,), jnp.int32),
            pltpu.VMEM((PAIR * GRAN, 2 * rank), jnp.float32),
            pltpu.VMEM((PAIR * GRAN, traces * rank), jnp.float32),
            pltpu.VMEM((2 * rank, traces * rank), jnp.float32),
            pltpu.SemaphoreType.DMA((2, RING)),
            pltpu.SemaphoreType.DMA((3,)),
        ],
        compiler_params=pltpu.CompilerParams(vmem_limit_bytes=40 << 20),
        cost_estimate=pl.CostEstimate(
            flops=2 * rows * rank * (width_dev + model),
            bytes_accessed=2 * rows * (width_dev + model),
            transcendentals=0,
        ),
        name="sketches",
    )(*(pltpu.with_memory_space_constraint(value, pltpu.HBM) for value in (lengths, hidden, grads, in_proj, out_proj)))


def score_kernel(traces, chip, keep, got, *rest):
    pieces, (own_out, other_out) = rest[:-2], rest[-2:]
    rank = keep.shape[1] // traces
    entries = pieces[0].shape[1]
    depth = entries // rank
    lane = lax.broadcasted_iota(jnp.int32, (depth, entries), 1) // rank
    diagonal = lane == lax.broadcasted_iota(jnp.int32, (depth, entries), 0)
    total = None
    for mask, piece in enumerate(pieces):
        rows = pl.ds(pl.multiple_of((chip[0] ^ mask) * depth, depth), depth)
        blocks = []
        for values in (keep[rows], got[rows]):
            for trace in range(traces):
                wide = jnp.concatenate([values[:, trace * rank : (trace + 1) * rank]] * depth, axis=1)
                blocks.append(jnp.where(diagonal, wide, 0.0))
        left = jnp.concatenate(blocks, axis=0).astype(jnp.bfloat16)
        term = lax.dot_general(left, piece[...], NT, preferred_element_type=jnp.float32)
        total = term if total is None else total + term
    sums = jnp.sum(total.reshape(2 * traces, depth, total.shape[1]), axis=1)
    own_out[...] = sums[:traces]
    other_out[...] = sums[traces:]


def exchange(value, axis, size, mask):
    return lax.ppermute(value, axis, [(i, i ^ mask) for i in range(size)])


def per_device(dp, width, hidden_inputs, output_grads, lengths, in_proj, out_proj, query_sketches):
    traces, _, _ = hidden_inputs.shape
    queries, entries = query_sketches.shape
    rank = in_proj.shape[0]
    depth = entries // rank
    place = lax.axis_index("dp")
    core, chip = place & 1, place >> 1
    pieces = [query_sketches] + [exchange(query_sketches, "dp", dp, 2 * mask) for mask in range(1, dp // 2)]

    packed = local_sketches(lengths, hidden_inputs, output_grads, in_proj, out_proj)
    for mask in [1 << bit for bit in range(width.bit_length() - 1)]:
        packed = packed + exchange(packed, "width", width, mask)
    packed, *pieces = lax.optimization_barrier((packed, *pieces))
    by_core = packed.reshape(dp // 2, 2, depth, traces * rank)
    even = by_core[:, 0].reshape(rank // 2, traces * rank)
    odd = by_core[:, 1].reshape(rank // 2, traces * rank)
    keep = jnp.where(core == 0, even, odd)
    got = exchange(jnp.where(core == 0, odd, even), "dp", dp, 1)

    scores = jax.ShapeDtypeStruct((traces, queries), jnp.float32)
    vmem = pl.BlockSpec(memory_space=pltpu.VMEM)
    own, other = pl.pallas_call(
        functools.partial(score_kernel, traces),
        out_shape=(scores, scores),
        in_specs=[pl.BlockSpec(memory_space=pltpu.SMEM)] + [vmem] * (2 + len(pieces)),
        out_specs=(vmem, vmem),
        compiler_params=pltpu.CompilerParams(vmem_limit_bytes=24 << 20),
        name="scores",
    )(chip.astype(jnp.int32).reshape(1), keep, got, *pieces)
    return own + exchange(other, "dp", dp, 1)


def solution(mesh):
    return jax.shard_map(
        functools.partial(per_device, mesh.shape["dp"], mesh.shape["width"]),
        mesh=mesh,
        in_specs=(
            P("dp", None, "width"),
            P("dp", None, None),
            P("dp"),
            P(None, "width"),
            P(),
            P(None, "dp"),
        ),
        out_specs=P("dp", None),
        check_vma=False,
    )
```

```python
import functools

import jax
import jax.numpy as jnp
from jax import lax
from jax.experimental import pallas as pl
from jax.experimental.pallas import tpu as pltpu
from jax.sharding import PartitionSpec as P

GRAN = 128
PAIR = 2
RING = 12

NT = (((1,), (1,)), ((), ()))
TN = (((0,), (0,)), ((), ()))


def split_bf16(value):
    high = value.astype(jnp.bfloat16)
    low = (value - high.astype(jnp.float32)).astype(jnp.bfloat16)
    return high, low


def sketch_kernel(
    lengths_hbm, hidden, grads, in_hbm, out_hbm, packed, hid_buf, grad_buf, in_proj, out_proj, lengths, in_last, out_last, total_ref, sems, once
):
    traces, length_dev, _ = hidden.shape
    rank = in_hbm.shape[0]

    def copies(slot, trace, row):
        rows = pl.ds(row, GRAN)
        return (
            pltpu.make_async_copy(hidden.at[trace, rows], hid_buf.at[slot], sems.at[0, slot]),
            pltpu.make_async_copy(grads.at[trace, rows], grad_buf.at[slot], sems.at[1, slot]),
        )

    fetch = [
        pltpu.make_async_copy(lengths_hbm, lengths, once.at[0]),
        pltpu.make_async_copy(in_hbm, in_proj.at[pl.ds(0, rank)], once.at[1]),
        pltpu.make_async_copy(out_hbm, out_proj.at[pl.ds(0, rank)], once.at[2]),
    ]
    for copy in fetch:
        copy.start()
    for index in range(PAIR):
        for copy in copies(index, 0, index * GRAN):
            copy.start()
    fetch[0].wait()
    counts = [jnp.minimum(lengths[i], length_dev) for i in range(traces)]
    firsts, total = [], 0
    for i in range(traces):
        firsts.append(total)
        total = total + (counts[i] + GRAN - 1) // GRAN

    def locate(index):
        trace, first, count = 0, 0, counts[0]
        for i in range(1, traces):
            later = index >= firsts[i]
            trace = jnp.where(later, i, trace)
            first = jnp.where(later, firsts[i], first)
            count = jnp.where(later, counts[i], count)
        return trace, pl.multiple_of((index - first) * GRAN, GRAN), count

    def start(index):
        @pl.when(index < total)
        def _():
            trace, row, _ = locate(index)
            for copy in copies(lax.rem(index, RING), trace, row):
                copy.start()

    for index in range(PAIR, RING):
        start(index)
    total_ref[...] = jnp.zeros_like(total_ref)
    in_last[...] = jnp.zeros_like(in_last)
    out_last[...] = jnp.zeros_like(out_last)
    for copy in fetch[1:]:
        copy.wait()
    in_proj[rank:] = in_proj[:rank]
    for i in range(1, traces):
        out_proj[i * rank : (i + 1) * rank] = out_proj[:rank]

    def project(index, parts):
        for part in range(parts):
            trace, row, _ = locate(index + part)
            for copy in copies(lax.rem(index + part, RING), trace, row):
                copy.wait()
        slots = pl.ds(lax.rem(index, RING), parts)
        hid_rows = hid_buf[slots].reshape(parts * GRAN, hid_buf.shape[2])
        grad_rows = grad_buf[slots].reshape(parts * GRAN, grad_buf.shape[2])
        in_side = lax.dot_general(hid_rows, in_proj[...], NT, preferred_element_type=jnp.float32)
        out_side = lax.dot_general(grad_rows, out_proj[...], NT, preferred_element_type=jnp.float32)
        return in_side, out_side

    def add(index, parts, in_side, out_side):
        block = lax.broadcasted_iota(jnp.int32, (GRAN, traces * rank), 1) // rank
        token = lax.broadcasted_iota(jnp.int32, (GRAN, traces * rank), 0)
        kept = []
        for part in range(parts):
            trace, row, count = locate(index + part)
            kept.append((block == trace) & (token + row < count))
        out_side = jnp.where(jnp.concatenate(kept, axis=0), out_side, 0.0)
        out_high, out_low = split_bf16(out_side)
        high = in_side.astype(jnp.bfloat16).astype(jnp.float32)
        first = lax.broadcasted_iota(jnp.int32, in_side.shape, 1) < rank
        both = jnp.where(first, high, in_side - high).astype(jnp.bfloat16)
        total_ref[...] += lax.dot_general(
            jnp.concatenate([both, both], axis=0),
            jnp.concatenate([out_high, out_low], axis=0),
            TN,
            preferred_element_type=jnp.float32,
        )

    def body(step, carry):
        index = step * PAIR
        in_before, out_before = in_last[...], out_last[...]
        in_side, out_side = project(index, PAIR)
        add(index - PAIR, PAIR, in_before, out_before)
        in_last[...] = in_side
        out_last[...] = out_side
        for part in range(PAIR):
            start(index + part + RING)
        return carry

    pairs = total // PAIR
    lax.fori_loop(0, pairs, body, 0)

    @pl.when(total % PAIR == 0)
    def _():
        add((pairs - 1) * PAIR, PAIR, in_last[...], out_last[...])

    @pl.when(total % PAIR != 0)
    def _():
        in_side, out_side = project(pairs * PAIR, 1)
        add((pairs - 1) * PAIR, PAIR, in_last[...], out_last[...])
        add(pairs * PAIR, 1, in_side, out_side)

    packed[...] = total_ref[:rank] + total_ref[rank:]


def local_sketches(lengths, hidden, grads, in_proj, out_proj):
    traces, length_dev, width_dev = hidden.shape
    rank, model = out_proj.shape
    rows = traces * length_dev
    return pl.pallas_call(
        sketch_kernel,
        out_shape=jax.ShapeDtypeStruct((rank, traces * rank), jnp.float32),
        in_specs=[pl.BlockSpec(memory_space=pltpu.HBM)] * 5,
        out_specs=pl.BlockSpec(memory_space=pltpu.VMEM),
        scratch_shapes=[
            pltpu.VMEM((RING, GRAN, width_dev), jnp.bfloat16),
            pltpu.VMEM((RING, GRAN, model), jnp.bfloat16),
            pltpu.VMEM((2 * rank, width_dev), jnp.bfloat16),
            pltpu.VMEM((traces * rank, model), jnp.bfloat16),
            pltpu.SMEM((traces,), jnp.int32),
            pltpu.VMEM((PAIR * GRAN, 2 * rank), jnp.float32),
            pltpu.VMEM((PAIR * GRAN, traces * rank), jnp.float32),
            pltpu.VMEM((2 * rank, traces * rank), jnp.float32),
            pltpu.SemaphoreType.DMA((2, RING)),
            pltpu.SemaphoreType.DMA((3,)),
        ],
        compiler_params=pltpu.CompilerParams(vmem_limit_bytes=40 << 20),
        cost_estimate=pl.CostEstimate(
            flops=2 * rows * rank * (width_dev + model),
            bytes_accessed=2 * rows * (width_dev + model),
            transcendentals=0,
        ),
        name="sketches",
    )(*(pltpu.with_memory_space_constraint(value, pltpu.HBM) for value in (lengths, hidden, grads, in_proj, out_proj)))


def score_kernel(traces, chip, keep, got, *rest):
    pieces, (own_out, other_out) = rest[:-2], rest[-2:]
    rank = keep.shape[1] // traces
    entries = pieces[0].shape[1]
    depth = entries // rank
    lane = lax.broadcasted_iota(jnp.int32, (depth, entries), 1) // rank
    diagonal = lane == lax.broadcasted_iota(jnp.int32, (depth, entries), 0)
    total = None
    for mask, piece in enumerate(pieces):
        rows = pl.ds(pl.multiple_of((chip[0] ^ mask) * depth, depth), depth)
        blocks = []
        for values in (keep[rows], got[rows]):
            for trace in range(traces):
                wide = jnp.concatenate([values[:, trace * rank : (trace + 1) * rank]] * depth, axis=1)
                blocks.append(jnp.where(diagonal, wide, 0.0))
        left = jnp.concatenate(blocks, axis=0).astype(jnp.bfloat16)
        term = lax.dot_general(left, piece[...], NT, preferred_element_type=jnp.float32)
        total = term if total is None else total + term
    sums = jnp.sum(total.reshape(2 * traces, depth, total.shape[1]), axis=1)
    own_out[...] = sums[:traces]
    other_out[...] = sums[traces:]


def exchange(value, axis, size, mask):
    return lax.ppermute(value, axis, [(i, i ^ mask) for i in range(size)])


def per_device(dp, width, hidden_inputs, output_grads, lengths, in_proj, out_proj, query_sketches):
    traces, _, _ = hidden_inputs.shape
    queries, entries = query_sketches.shape
    rank = in_proj.shape[0]
    depth = entries // rank
    place = lax.axis_index("dp")
    core, chip = place & 1, place >> 1
    pieces = [query_sketches] + [exchange(query_sketches, "dp", dp, 2 * mask) for mask in range(1, dp // 2)]

    packed = local_sketches(lengths, hidden_inputs, output_grads, in_proj, out_proj)
    packed, *pieces[:-1] = lax.optimization_barrier((packed, *pieces[:-1]))
    packed = sum([packed] + [exchange(packed, "width", width, mask) for mask in range(1, width)])
    packed, pieces[-1] = lax.optimization_barrier((packed, pieces[-1]))
    by_core = packed.reshape(dp // 2, 2, depth, traces * rank)
    even = by_core[:, 0].reshape(rank // 2, traces * rank)
    odd = by_core[:, 1].reshape(rank // 2, traces * rank)
    keep = jnp.where(core == 0, even, odd)
    got = exchange(jnp.where(core == 0, odd, even), "dp", dp, 1)

    scores = jax.ShapeDtypeStruct((traces, queries), jnp.float32)
    vmem = pl.BlockSpec(memory_space=pltpu.VMEM)
    own, other = pl.pallas_call(
        functools.partial(score_kernel, traces),
        out_shape=(scores, scores),
        in_specs=[pl.BlockSpec(memory_space=pltpu.SMEM)] + [vmem] * (2 + len(pieces)),
        out_specs=(vmem, vmem),
        compiler_params=pltpu.CompilerParams(vmem_limit_bytes=24 << 20),
        name="scores",
    )(chip.astype(jnp.int32).reshape(1), keep, got, *pieces)
    return own + exchange(other, "dp", dp, 1)


def solution(mesh):
    return jax.shard_map(
        functools.partial(per_device, mesh.shape["dp"], mesh.shape["width"]),
        mesh=mesh,
        in_specs=(
            P("dp", None, "width"),
            P("dp", None, None),
            P("dp"),
            P(None, "width"),
            P(),
            P(None, "dp"),
        ),
        out_specs=P("dp", None),
        check_vma=False,
    )
```

```python
import functools

import jax
import jax.numpy as jnp
from jax import lax
from jax.experimental import pallas as pl
from jax.experimental.pallas import tpu as pltpu
from jax.sharding import PartitionSpec as P

GRAN = 128
STEP = 2
SLOTS = 6
RING = STEP * SLOTS

NT = (((1,), (1,)), ((), ()))
TN = (((0,), (0,)), ((), ()))


def split_bf16(value):
    high = value.astype(jnp.bfloat16)
    low = (value - high.astype(jnp.float32)).astype(jnp.bfloat16)
    return high, low


def sketch_kernel(
    lengths_hbm, hidden, grads, in_hbm, out_hbm, packed, hid_buf, grad_buf, in_proj, out_proj, lengths, in_last, out_last, total_ref, sems, once
):
    traces, length_dev, _ = hidden.shape
    rank = in_hbm.shape[0]

    def start(index, trace, row):
        rows, slot = pl.ds(row, GRAN), lax.rem(index, RING)
        group = slot // STEP
        pltpu.make_async_copy(hidden.at[trace, rows], hid_buf.at[slot], sems.at[0, group]).start()
        pltpu.make_async_copy(grads.at[trace, rows], grad_buf.at[slot], sems.at[1, group]).start()

    fetch = [
        pltpu.make_async_copy(lengths_hbm, lengths, once.at[0]),
        pltpu.make_async_copy(in_hbm, in_proj.at[pl.ds(0, rank)], once.at[1]),
        pltpu.make_async_copy(out_hbm, out_proj.at[pl.ds(0, rank)], once.at[2]),
    ]
    for copy in fetch:
        copy.start()
    for index in range(STEP):
        start(index, 0, index * GRAN)
    fetch[0].wait()
    counts = [jnp.minimum(lengths[i], length_dev) for i in range(traces)]
    firsts, total = [], 0
    for i in range(traces):
        firsts.append(total)
        total = total + (counts[i] + GRAN - 1) // GRAN

    def locate(index):
        trace, first, count = 0, 0, counts[0]
        for i in range(1, traces):
            later = index >= firsts[i]
            trace = jnp.where(later, i, trace)
            first = jnp.where(later, firsts[i], first)
            count = jnp.where(later, counts[i], count)
        return trace, pl.multiple_of((index - first) * GRAN, GRAN), count

    def start_step(index):
        @pl.when(index + STEP <= total)
        def _():
            for part in range(STEP):
                trace, row, _ = locate(index + part)
                start(index + part, trace, row)

        @pl.when((index < total) & (index + STEP > total))
        def _():
            for part in range(STEP - 1):

                @pl.when(index + part < total)
                def _():
                    trace, row, _ = locate(index + part)
                    start(index + part, trace, row)

    for index in range(STEP, RING, STEP):
        start_step(index)
    total_ref[...] = jnp.zeros_like(total_ref)
    in_last[...] = jnp.zeros_like(in_last)
    out_last[...] = jnp.zeros_like(out_last)
    for copy in fetch[1:]:
        copy.wait()
    in_proj[rank:] = in_proj[:rank]
    for i in range(1, traces):
        out_proj[i * rank : (i + 1) * rank] = out_proj[:rank]

    def project(index, parts):
        first = pl.multiple_of(lax.rem(index, RING), STEP)
        slots, group = pl.ds(first, parts), first // STEP
        pltpu.make_async_copy(hid_buf.at[slots], hid_buf.at[slots], sems.at[0, group]).wait()
        pltpu.make_async_copy(grad_buf.at[slots], grad_buf.at[slots], sems.at[1, group]).wait()
        hid_rows = hid_buf[slots].reshape(parts * GRAN, hid_buf.shape[2])
        grad_rows = grad_buf[slots].reshape(parts * GRAN, grad_buf.shape[2])
        in_side = lax.dot_general(hid_rows, in_proj[...], NT, preferred_element_type=jnp.float32)
        out_side = lax.dot_general(grad_rows, out_proj[...], NT, preferred_element_type=jnp.float32)
        return in_side, out_side

    def add(index, parts, in_side, out_side):
        block = lax.broadcasted_iota(jnp.int32, (GRAN, traces * rank), 1) // rank
        token = lax.broadcasted_iota(jnp.int32, (GRAN, traces * rank), 0)
        kept = []
        for part in range(parts):
            trace, row, count = locate(index + part)
            kept.append((block == trace) & (token + row < count))
        out_side = jnp.where(jnp.concatenate(kept, axis=0), out_side, 0.0)
        out_high, out_low = split_bf16(out_side)
        high = in_side.astype(jnp.bfloat16).astype(jnp.float32)
        first = lax.broadcasted_iota(jnp.int32, in_side.shape, 1) < rank
        both = jnp.where(first, high, in_side - high).astype(jnp.bfloat16)
        total_ref[...] += lax.dot_general(
            both,
            jnp.concatenate([out_high, out_low], axis=1),
            TN,
            preferred_element_type=jnp.float32,
        )

    def body(step, carry):
        index = step * STEP
        in_before, out_before = in_last[...], out_last[...]
        in_side, out_side = project(index, STEP)
        add(index - STEP, STEP, in_before, out_before)
        in_last[...] = in_side
        out_last[...] = out_side
        start_step(index + RING)
        return carry

    steps = total // STEP
    lax.fori_loop(0, steps, body, 0)
    last = steps * STEP
    for left in range(STEP):

        @pl.when(total - last == left)
        def _():
            sides = project(last, left) if left else None
            add(last - STEP, STEP, in_last[...], out_last[...])
            if left:
                add(last, left, *sides)

    sums = total_ref[:rank] + total_ref[rank:]
    packed[...] = sums[:, : traces * rank] + sums[:, traces * rank :]


def local_sketches(lengths, hidden, grads, in_proj, out_proj):
    traces, length_dev, width_dev = hidden.shape
    rank, model = out_proj.shape
    rows = traces * length_dev
    return pl.pallas_call(
        sketch_kernel,
        out_shape=jax.ShapeDtypeStruct((rank, traces * rank), jnp.float32),
        in_specs=[pl.BlockSpec(memory_space=pltpu.HBM)] * 5,
        out_specs=pl.BlockSpec(memory_space=pltpu.VMEM),
        scratch_shapes=[
            pltpu.VMEM((RING, GRAN, width_dev), jnp.bfloat16),
            pltpu.VMEM((RING, GRAN, model), jnp.bfloat16),
            pltpu.VMEM((2 * rank, width_dev), jnp.bfloat16),
            pltpu.VMEM((traces * rank, model), jnp.bfloat16),
            pltpu.SMEM((traces,), jnp.int32),
            pltpu.VMEM((STEP * GRAN, 2 * rank), jnp.float32),
            pltpu.VMEM((STEP * GRAN, traces * rank), jnp.float32),
            pltpu.VMEM((2 * rank, 2 * traces * rank), jnp.float32),
            pltpu.SemaphoreType.DMA((2, SLOTS)),
            pltpu.SemaphoreType.DMA((3,)),
        ],
        compiler_params=pltpu.CompilerParams(vmem_limit_bytes=40 << 20),
        cost_estimate=pl.CostEstimate(
            flops=2 * rows * rank * (width_dev + model),
            bytes_accessed=2 * rows * (width_dev + model),
            transcendentals=0,
        ),
        name="sketches",
    )(*(pltpu.with_memory_space_constraint(value, pltpu.HBM) for value in (lengths, hidden, grads, in_proj, out_proj)))


def score_kernel(traces, chip, keep, got, *rest):
    pieces, (own_out, other_out) = rest[:-2], rest[-2:]
    rank = keep.shape[1] // traces
    entries = pieces[0].shape[1]
    depth = entries // rank
    lane = lax.broadcasted_iota(jnp.int32, (depth, entries), 1) // rank
    diagonal = lane == lax.broadcasted_iota(jnp.int32, (depth, entries), 0)
    total = None
    for mask, piece in enumerate(pieces):
        rows = pl.ds(pl.multiple_of((chip[0] ^ mask) * depth, depth), depth)
        blocks = []
        for values in (keep[rows], got[rows]):
            for trace in range(traces):
                wide = jnp.concatenate([values[:, trace * rank : (trace + 1) * rank]] * depth, axis=1)
                blocks.append(jnp.where(diagonal, wide, 0.0))
        left = jnp.concatenate(blocks, axis=0).astype(jnp.bfloat16)
        term = lax.dot_general(left, piece[...], NT, preferred_element_type=jnp.float32)
        total = term if total is None else total + term
    sums = jnp.sum(total.reshape(2 * traces, depth, total.shape[1]), axis=1)
    own_out[...] = sums[:traces]
    other_out[...] = sums[traces:]


def exchange(value, axis, size, mask):
    return lax.ppermute(value, axis, [(i, i ^ mask) for i in range(size)])


def per_device(dp, width, hidden_inputs, output_grads, lengths, in_proj, out_proj, query_sketches):
    traces, _, _ = hidden_inputs.shape
    queries, entries = query_sketches.shape
    rank = in_proj.shape[0]
    depth = entries // rank
    place = lax.axis_index("dp")
    core, chip = place & 1, place >> 1
    pieces = [query_sketches] + [exchange(query_sketches, "dp", dp, 2 * mask) for mask in range(1, dp // 2)]

    packed = local_sketches(lengths, hidden_inputs, output_grads, in_proj, out_proj)
    packed, *pieces[:-1] = lax.optimization_barrier((packed, *pieces[:-1]))
    packed = sum([packed] + [exchange(packed, "width", width, mask) for mask in range(1, width)])
    packed, pieces[-1] = lax.optimization_barrier((packed, pieces[-1]))
    by_core = packed.reshape(dp // 2, 2, depth, traces * rank)
    even = by_core[:, 0].reshape(rank // 2, traces * rank)
    odd = by_core[:, 1].reshape(rank // 2, traces * rank)
    keep = jnp.where(core == 0, even, odd)
    got = exchange(jnp.where(core == 0, odd, even), "dp", dp, 1)

    scores = jax.ShapeDtypeStruct((traces, queries), jnp.float32)
    vmem = pl.BlockSpec(memory_space=pltpu.VMEM)
    own, other = pl.pallas_call(
        functools.partial(score_kernel, traces),
        out_shape=(scores, scores),
        in_specs=[pl.BlockSpec(memory_space=pltpu.SMEM)] + [vmem] * (2 + len(pieces)),
        out_specs=(vmem, vmem),
        compiler_params=pltpu.CompilerParams(vmem_limit_bytes=24 << 20),
        name="scores",
    )(chip.astype(jnp.int32).reshape(1), keep, got, *pieces)
    return own + exchange(other, "dp", dp, 1)


def solution(mesh):
    return jax.shard_map(
        functools.partial(per_device, mesh.shape["dp"], mesh.shape["width"]),
        mesh=mesh,
        in_specs=(
            P("dp", None, "width"),
            P("dp", None, None),
            P("dp"),
            P(None, "width"),
            P(),
            P(None, "dp"),
        ),
        out_specs=P("dp", None),
        check_vma=False,
    )
```

```python
import functools

import jax
import jax.numpy as jnp
from jax import lax
from jax.experimental import pallas as pl
from jax.experimental.pallas import tpu as pltpu
from jax.sharding import PartitionSpec as P

GRAN = 128
STEP = 2
SLOTS = 6
RING = STEP * SLOTS

NT = (((1,), (1,)), ((), ()))
TN = (((0,), (0,)), ((), ()))


def split_bf16(value):
    high = value.astype(jnp.bfloat16)
    low = (value - high.astype(jnp.float32)).astype(jnp.bfloat16)
    return high, low


def sketch_kernel(
    lengths_hbm, hidden, grads, in_hbm, out_hbm, packed, hid_buf, grad_buf, in_proj, out_proj, lengths, in_last, out_last, total_ref, sems, once
):
    traces, length_dev, _ = hidden.shape
    rank = in_hbm.shape[0]

    def start(index, trace, row):
        rows, slot = pl.ds(row, GRAN), lax.rem(index, RING)
        group = slot // STEP
        pltpu.make_async_copy(hidden.at[trace, rows], hid_buf.at[slot], sems.at[0, group]).start()
        pltpu.make_async_copy(grads.at[trace, rows], grad_buf.at[slot], sems.at[1, group]).start()

    fetch = [
        pltpu.make_async_copy(lengths_hbm, lengths, once.at[0]),
        pltpu.make_async_copy(in_hbm, in_proj.at[pl.ds(0, rank)], once.at[1]),
        pltpu.make_async_copy(out_hbm, out_proj.at[pl.ds(0, rank)], once.at[2]),
    ]
    for copy in fetch:
        copy.start()
    for index in range(STEP):
        start(index, 0, index * GRAN)
    fetch[0].wait()
    counts = [jnp.minimum(lengths[i], length_dev) for i in range(traces)]
    firsts, total = [], 0
    for i in range(traces):
        firsts.append(total)
        total = total + (counts[i] + GRAN - 1) // GRAN

    def locate(index):
        trace, first, count = 0, 0, counts[0]
        for i in range(1, traces):
            later = index >= firsts[i]
            trace = jnp.where(later, i, trace)
            first = jnp.where(later, firsts[i], first)
            count = jnp.where(later, counts[i], count)
        return trace, pl.multiple_of((index - first) * GRAN, GRAN), count

    def start_step(index):
        @pl.when(index + STEP <= total)
        def _():
            for part in range(STEP):
                trace, row, _ = locate(index + part)
                start(index + part, trace, row)

        @pl.when((index < total) & (index + STEP > total))
        def _():
            for part in range(STEP - 1):

                @pl.when(index + part < total)
                def _():
                    trace, row, _ = locate(index + part)
                    start(index + part, trace, row)

    for index in range(STEP, RING, STEP):
        start_step(index)
    total_ref[...] = jnp.zeros_like(total_ref)
    in_last[...] = jnp.zeros_like(in_last)
    out_last[...] = jnp.zeros_like(out_last)
    for copy in fetch[1:]:
        copy.wait()
    in_proj[rank:] = in_proj[:rank]
    for i in range(1, traces):
        out_proj[i * rank : (i + 1) * rank] = out_proj[:rank]

    def project(index, parts):
        first = pl.multiple_of(lax.rem(index, RING), STEP)
        slots, group = pl.ds(first, parts), first // STEP
        pltpu.make_async_copy(hid_buf.at[slots], hid_buf.at[slots], sems.at[0, group]).wait()
        pltpu.make_async_copy(grad_buf.at[slots], grad_buf.at[slots], sems.at[1, group]).wait()
        hid_rows = hid_buf[slots].reshape(parts * GRAN, hid_buf.shape[2])
        grad_rows = grad_buf[slots].reshape(parts * GRAN, grad_buf.shape[2])
        in_side = lax.dot_general(hid_rows, in_proj[...], NT, preferred_element_type=jnp.float32)
        out_side = lax.dot_general(grad_rows, out_proj[...], NT, preferred_element_type=jnp.float32)
        return in_side, out_side

    def add(index, parts, in_side, out_side):
        block = lax.broadcasted_iota(jnp.int32, (1, traces * rank), 1) // rank
        token = lax.broadcasted_iota(jnp.int32, (GRAN, traces * rank), 0)
        kept = []
        for part in range(parts):
            trace, row, count = locate(index + part)
            kept.append(token < jnp.where(block == trace, count - row, 0))
        out_side = jnp.where(jnp.concatenate(kept, axis=0), out_side, 0.0)
        out_high, out_low = split_bf16(out_side)
        high = in_side.astype(jnp.bfloat16).astype(jnp.float32)
        first = lax.broadcasted_iota(jnp.int32, in_side.shape, 1) < rank
        both = jnp.where(first, high, in_side - high).astype(jnp.bfloat16)
        total_ref[...] += lax.dot_general(
            both,
            jnp.concatenate([out_high, out_low], axis=1),
            TN,
            preferred_element_type=jnp.float32,
        )

    def body(step, carry):
        index = step * STEP
        in_before, out_before = in_last[...], out_last[...]
        in_side, out_side = project(index, STEP)
        add(index - STEP, STEP, in_before, out_before)
        in_last[...] = in_side
        out_last[...] = out_side
        start_step(index + RING)
        return carry

    steps = total // STEP
    lax.fori_loop(0, steps, body, 0)
    last = steps * STEP
    for left in range(STEP):

        @pl.when(total - last == left)
        def _():
            sides = project(last, left) if left else None
            add(last - STEP, STEP, in_last[...], out_last[...])
            if left:
                add(last, left, *sides)

    sums = total_ref[:rank] + total_ref[rank:]
    packed[...] = sums[:, : traces * rank] + sums[:, traces * rank :]


def local_sketches(lengths, hidden, grads, in_proj, out_proj):
    traces, length_dev, width_dev = hidden.shape
    rank, model = out_proj.shape
    rows = traces * length_dev
    return pl.pallas_call(
        sketch_kernel,
        out_shape=jax.ShapeDtypeStruct((rank, traces * rank), jnp.float32),
        in_specs=[pl.BlockSpec(memory_space=pltpu.HBM)] * 5,
        out_specs=pl.BlockSpec(memory_space=pltpu.VMEM),
        scratch_shapes=[
            pltpu.VMEM((RING, GRAN, width_dev), jnp.bfloat16),
            pltpu.VMEM((RING, GRAN, model), jnp.bfloat16),
            pltpu.VMEM((2 * rank, width_dev), jnp.bfloat16),
            pltpu.VMEM((traces * rank, model), jnp.bfloat16),
            pltpu.SMEM((traces,), jnp.int32),
            pltpu.VMEM((STEP * GRAN, 2 * rank), jnp.float32),
            pltpu.VMEM((STEP * GRAN, traces * rank), jnp.float32),
            pltpu.VMEM((2 * rank, 2 * traces * rank), jnp.float32),
            pltpu.SemaphoreType.DMA((2, SLOTS)),
            pltpu.SemaphoreType.DMA((3,)),
        ],
        compiler_params=pltpu.CompilerParams(vmem_limit_bytes=40 << 20),
        cost_estimate=pl.CostEstimate(
            flops=2 * rows * rank * (width_dev + model),
            bytes_accessed=2 * rows * (width_dev + model),
            transcendentals=0,
        ),
        name="sketches",
    )(*(pltpu.with_memory_space_constraint(value, pltpu.HBM) for value in (lengths, hidden, grads, in_proj, out_proj)))


def score_kernel(traces, chip, keep, got, *rest):
    pieces, (own_out, other_out) = rest[:-2], rest[-2:]
    rank = keep.shape[1] // traces
    entries = pieces[0].shape[1]
    depth = entries // rank
    lane = lax.broadcasted_iota(jnp.int32, (depth, entries), 1) // rank
    diagonal = lane == lax.broadcasted_iota(jnp.int32, (depth, entries), 0)
    total = None
    for mask, piece in enumerate(pieces):
        rows = pl.ds(pl.multiple_of((chip[0] ^ mask) * depth, depth), depth)
        blocks = []
        for values in (keep[rows], got[rows]):
            for trace in range(traces):
                wide = jnp.concatenate([values[:, trace * rank : (trace + 1) * rank]] * depth, axis=1)
                blocks.append(jnp.where(diagonal, wide, 0.0))
        left = jnp.concatenate(blocks, axis=0).astype(jnp.bfloat16)
        term = lax.dot_general(left, piece[...], NT, preferred_element_type=jnp.float32)
        total = term if total is None else total + term
    sums = jnp.sum(total.reshape(2 * traces, depth, total.shape[1]), axis=1)
    own_out[...] = sums[:traces]
    other_out[...] = sums[traces:]


def exchange(value, axis, size, mask):
    return lax.ppermute(value, axis, [(i, i ^ mask) for i in range(size)])


def per_device(dp, width, hidden_inputs, output_grads, lengths, in_proj, out_proj, query_sketches):
    traces, _, _ = hidden_inputs.shape
    queries, entries = query_sketches.shape
    rank = in_proj.shape[0]
    depth = entries // rank
    place = lax.axis_index("dp")
    core, chip = place & 1, place >> 1
    pieces = [query_sketches] + [exchange(query_sketches, "dp", dp, 2 * mask) for mask in range(1, dp // 2)]

    packed = local_sketches(lengths, hidden_inputs, output_grads, in_proj, out_proj)
    packed, *pieces[:-1] = lax.optimization_barrier((packed, *pieces[:-1]))
    packed = sum([packed] + [exchange(packed, "width", width, mask) for mask in range(1, width)])
    packed, pieces[-1] = lax.optimization_barrier((packed, pieces[-1]))
    by_core = packed.reshape(dp // 2, 2, depth, traces * rank)
    even = by_core[:, 0].reshape(rank // 2, traces * rank)
    odd = by_core[:, 1].reshape(rank // 2, traces * rank)
    keep = jnp.where(core == 0, even, odd)
    got = exchange(jnp.where(core == 0, odd, even), "dp", dp, 1)

    scores = jax.ShapeDtypeStruct((traces, queries), jnp.float32)
    vmem = pl.BlockSpec(memory_space=pltpu.VMEM)
    own, other = pl.pallas_call(
        functools.partial(score_kernel, traces),
        out_shape=(scores, scores),
        in_specs=[pl.BlockSpec(memory_space=pltpu.SMEM)] + [vmem] * (2 + len(pieces)),
        out_specs=(vmem, vmem),
        compiler_params=pltpu.CompilerParams(vmem_limit_bytes=24 << 20),
        name="scores",
    )(chip.astype(jnp.int32).reshape(1), keep, got, *pieces)
    return own + exchange(other, "dp", dp, 1)


def solution(mesh):
    return jax.shard_map(
        functools.partial(per_device, mesh.shape["dp"], mesh.shape["width"]),
        mesh=mesh,
        in_specs=(
            P("dp", None, "width"),
            P("dp", None, None),
            P("dp"),
            P(None, "width"),
            P(),
            P(None, "dp"),
        ),
        out_specs=P("dp", None),
        check_vma=False,
    )
```
